128 devices in a mesh: wide: 32 (over y, x, z_hi), blk: 4 (over z_lo, core).
Axes of the slice: x: 4, y: 4, z: 4 (z_hi: 2, z_lo: 2; z = z_hi * 2 + z_lo), core: 2. Of those that a mesh axis runs over, the one named last changes fastest.
Arguments:
- visual_features: bfloat16 [131072, 1152], P(('wide', 'blk')), may hold values from -0.1875 to 0.1875
- sentence_features: bfloat16 [4096, 1152], P(('wide', 'blk')), may hold values from -0.1875 to 0.1875
- true_partner_ids: int32 [131072], P(('wide', 'blk')), may hold values from 0 to 4095
- inverse_warmth: float32 [], replicated, may hold values from 90 to 110
- additive_adjust: float32 [], replicated, may hold values from -12 to -9
Outputs:
- grad_images: float32 [131072, 1152], P(('wide', 'blk'))
- grad_texts: float32 [4096, 1152], P(('wide', 'blk'))
The draws below stay inside these ranges and needn't reach their ends.
Inputs may be any that keep to these rules, and one draw needn't show every extreme that they name: Image i is paired with text true_partner_ids[i]; a text may be paired with several images or none.
All inputs are finite; a program needn't handle non-finite values.
Results may differ from the reference program's by a relative error of at most 0.007.
Values may be sent and summed in bfloat16 or wider, within the bound.
A program may use at most 64 MiB of HBM per device.

```python
import jax
import jax.numpy as jnp
from jax import lax

D = 1152
IMG_DEV = 1024
IMAGES = 131072
TEXTS = 4096


def with_ends(array, rng, smallest, high):
    longest = array.shape.index(max(array.shape))
    spots = []
    for shift in (0, 1):
        where = [jax.random.randint(jax.random.fold_in(rng, axis), (), 0, length) for axis, length in enumerate(array.shape)]
        where[longest] = (where[longest] + shift) % array.shape[longest]
        spots.append(tuple(where))
    return array.at[spots[0]].set(smallest).at[spots[1]].set(high)


def steps_of(stream_key, shape, cuts, least, largest):
    gain, own = 1.0, jax.random.fold_in(stream_key, 6)
    for axis_at, shards_of in cuts:
        draws = jnp.exp(jax.random.uniform(jax.random.fold_in(own, axis_at), (shards_of,), jnp.float32, least / len(cuts), largest / len(cuts)))
        gain = gain * jnp.repeat(draws, shape[axis_at] // shards_of).reshape([-1 if axis == axis_at else 1 for axis in range(len(shape))])
    return gain


def scatter_about(key, shape, width, bound, shards=(), kind=jnp.bfloat16):
    gain = steps_of(key, shape, shards, -0.22, 0.18) if shards else 1.0
    values = jax.random.normal(key, shape, jnp.float32) * width * gain
    return jnp.minimum(jnp.maximum(values, -bound), bound).astype(kind)


def setup_inputs(seed: int = 0) -> dict:
    arg_keys = jax.random.split(jax.random.key(seed), 6)
    return {
        "visual_features": scatter_about(arg_keys[0], (IMAGES, D), D ** -0.5, 0.1875, ((0, 128),)),
        "sentence_features": scatter_about(arg_keys[1], (TEXTS, D), D ** -0.5, 0.1875, ((0, 128),)),
        "true_partner_ids": with_ends(jax.random.randint(arg_keys[2], (IMAGES,), 0, TEXTS), jax.random.fold_in(arg_keys[2], 1), 0, TEXTS - 1).astype(jnp.int32),
        "inverse_warmth": jnp.clip(jax.random.uniform(arg_keys[3], (), jnp.float32, 90.0, 110.0), 90.0, 110.0),
        "additive_adjust": jnp.clip(jax.random.uniform(arg_keys[4], (), jnp.float32, -12.0, -9.0), -12.0, -9.0),
    }


def piecewise_updates(visual_part, aligned_text_part, sentence_features, inverse_warmth, additive_adjust):
    cosine_grid = jnp.dot(visual_part, sentence_features.T, preferred_element_type=jnp.float32)
    sigmoid_levels = inverse_warmth * cosine_grid + additive_adjust
    columns = jnp.arange(sentence_features.shape[0], dtype=jnp.int32)
    plus_minus_ones = jnp.where(aligned_text_part[:, None] == columns[None, :], 1.0, -1.0).astype(sigmoid_levels.dtype)
    loss_grid_scaled = (-inverse_warmth * plus_minus_ones * jax.nn.sigmoid(-plus_minus_ones * sigmoid_levels)).astype(jnp.bfloat16)
    incoming_grad_part = jnp.dot(loss_grid_scaled, sentence_features, preferred_element_type=jnp.float32)
    returned_grad_part = jnp.dot(loss_grid_scaled.T, visual_part, preferred_element_type=jnp.float32)
    return incoming_grad_part, returned_grad_part


def reference(visual_features, sentence_features, true_partner_ids, inverse_warmth, additive_adjust):
    count = visual_features.shape[0] // IMG_DEV
    img_blocks = visual_features.reshape(count, IMG_DEV, visual_features.shape[1])
    pair_blocks = true_partner_ids.reshape(count, IMG_DEV)

    def scan_step(carry, running_dot_sums):
        incoming_grad_part, returned_grad_part = piecewise_updates(running_dot_sums[0], running_dot_sums[1], sentence_features, inverse_warmth, additive_adjust)
        return carry + returned_grad_part, incoming_grad_part

    start = jnp.zeros(sentence_features.shape, jnp.float32)
    grad_texts, grad_blocks = lax.scan(scan_step, start, (img_blocks, pair_blocks))
    grad_images = grad_blocks.reshape(visual_features.shape)
    return grad_images, grad_texts
```

```python
import jax
import jax.numpy as jnp
from jax import lax
from jax.sharding import PartitionSpec as P

AXES = ("wide", "blk")


def shards(images, texts, partners, scale, bias):
    joined = lax.all_gather(texts, AXES, axis=0, tiled=True)
    scores = lax.dot_general(
        images, joined, (((1,), (1,)), ((), ())), preferred_element_type=jnp.float32
    )
    logits = scale * scores + bias
    columns = lax.iota(jnp.int32, joined.shape[0])
    sign = jnp.where(partners[:, None] == columns[None, :], 1.0, -1.0).astype(jnp.float32)
    weights = (-scale * sign * jax.nn.sigmoid(-sign * logits)).astype(jnp.bfloat16)
    grad_images = jnp.dot(weights, joined, preferred_element_type=jnp.float32)
    part = lax.dot_general(
        weights, images, (((0,), (0,)), ((), ())), preferred_element_type=jnp.float32
    )
    grad_texts = lax.psum_scatter(
        part.astype(jnp.bfloat16), AXES, scatter_dimension=0, tiled=True
    ).astype(jnp.float32)
    return grad_images, grad_texts


def solution(mesh):
    return jax.shard_map(
        shards,
        mesh=mesh,
        in_specs=(P(AXES, None), P(AXES, None), P(AXES), P(), P()),
        out_specs=(P(AXES, None), P(AXES, None)),
        check_vma=False,
    )
```

```python
import functools

import jax
import jax.numpy as jnp
from jax import lax
from jax.experimental import pallas as pl
from jax.experimental.pallas import tpu as pltpu
from jax.sharding import PartitionSpec as P

AXES = ("wide", "blk")
MESH = pl.DeviceIdType.MESH
LOG2E = 1.4426950408889634
ORDERS = ((2, 1, 0), (1, 0, 2), (0, 2, 1))
ALL = slice(None)


def here():
    w, b = lax.axis_index("wide"), lax.axis_index("blk")
    return ((w % 2) * 2 + b // 2, w // 8, (w // 2) % 4), b % 2


def device(zyx, core):
    z, y, x = zyx
    return (y * 8 + x * 2 + z // 2, (z % 2) * 2 + core)


def kernel(
    lag,
    scale_ref, bias_ref, ids_ref, images_ref, texts_ref,
    gi_out, gt_out,
    V, T, GI, GT, RB, R1, S1, R2, S2, R3, IDS, IDR, OUT,
    in_sem, v_send, v_recv, id_send, id_recv, gi_send, gi_recv, out_sem,
    a1_send, a1_recv, a2_send, a2_recv, a3_send, a3_recv,
    r1_send, r1_recv, r2_send, r2_recv, r3_send, r3_recv,
):
    me, core = here()
    rows = images_ref.shape[0]
    third = texts_ref.shape[1] // 3
    tdev = texts_ref.shape[0]
    chunk = 8 * tdev
    sibling = device(me, 1 - core)

    def shifted(axis, by):
        pos = list(me)
        pos[axis] = (pos[axis] + by + 4) % 4
        return device(pos, core)

    def part(ref, p, par, half):
        return ref.at[(*par, *half, ALL, pl.ds(p * third, third))]

    def put(axis, offset, seq):
        seq = list(seq)
        seq[axis] = offset
        return tuple(seq)

    own_v = pltpu.make_async_copy(images_ref, V.at[pl.ds(0, rows)], in_sem.at[0])
    own_t = pltpu.make_async_copy(texts_ref, T.at[0, 0, 0, 0, 0, 0], in_sem.at[1])
    own_v.start()
    own_t.start()

    barrier = pltpu.get_barrier_semaphore()
    pl.semaphore_signal(barrier, inc=1, device_id=sibling, device_id_type=MESH)
    for axis in range(3):
        for e in (1, 2, 3):
            pl.semaphore_signal(barrier, inc=1, device_id=shifted(axis, e), device_id_type=MESH)
    pl.semaphore_wait(barrier, 10)

    def remote(src, dst, send, recv, to):
        return pltpu.make_async_remote_copy(
            src_ref=src, dst_ref=dst, send_sem=send, recv_sem=recv, device_id=to, device_id_type=MESH
        )

    own_t.wait()
    light, middle = [], []
    for p, (a1, a2, a3) in enumerate(ORDERS):
        for e in (1, 2, 3):
            zero = (0, 0, 0)
            cp = remote(
                part(T, p, zero, zero),
                part(T, p, put(a1, e % 2, zero), put(a1, e // 2, zero)),
                a1_send.at[p, e - 1], a1_recv.at[p, e - 1], shifted(a1, -e),
            )
            cp.start()
            light.append(cp)

    send_v = remote(images_ref, V.at[pl.ds(rows, rows)], v_send, v_recv, sibling)
    send_v.start()
    send_ids = remote(ids_ref, IDS, id_send, id_recv, sibling)
    send_ids.start()

    for p, (a1, a2, a3) in enumerate(ORDERS):
        for e in (1, 2, 3):
            light[3 * p + e - 1].wait_recv()
        for e in (1, 2, 3):
            along = put(a1, ALL, (0, 0, 0))
            cp = remote(
                part(T, p, along, along),
                part(T, p, put(a2, e % 2, along), put(a2, e // 2, along)),
                a2_send.at[p, e - 1], a2_recv.at[p, e - 1], shifted(a2, -e),
            )
            cp.start()
            middle.append(cp)

    GI[...] = jnp.zeros_like(GI)

    def heavy_gather(p, r, half):
        a3 = ORDERS[p][2]
        e = r[a3] + 2 * half
        both = put(a3, 0, (ALL, ALL, ALL))
        return remote(
            part(T, p, put(a3, 0, r), both),
            part(T, p, r, put(a3, half, both)),
            a3_send.at[p, 4 * r[0] + 2 * r[1] + r[2], half],
            a3_recv.at[p, 4 * r[0] + 2 * r[1] + r[2], half],
            shifted(a3, -e),
        )

    for p in range(3):
        for e in (1, 2, 3):
            middle[3 * p + e - 1].wait_recv()
    for n in range(8):
        r = (n // 4, (n // 2) % 2, n % 2)
        for p in range(3):
            for half in (0, 1):
                if r[ORDERS[p][2]] + 2 * half:
                    heavy_gather(p, r, half).start()

    send_ids.wait_recv()
    for i in range(rows // 128):
        IDR[:, pl.ds(i * 128, 128)] = ids_ref[pl.ds(i, 1), :]
        IDR[:, pl.ds(rows + i * 128, 128)] = IDS[pl.ds(i, 1), :]
    own_v.wait()
    send_v.wait_recv()

    scale = scale_ref[0, 0]
    slope = -scale * LOG2E
    shift = -bias_ref[0, 0] * LOG2E

    def parities(n):
        return (n // 4, (n // 2) % 2, n % 2)

    def heavy_reduce(p, n, half):
        r = parities(n)
        a3 = ORDERS[p][2]
        e = r[a3] + 2 * half
        both = put(a3, half, (ALL, ALL, ALL))
        rest = [r[i] for i in range(3) if i != a3]
        return remote(
            part(GT, p, r, both),
            R1.at[p, e - 1, rest[0], rest[1]],
            r1_send.at[p, n, half], r1_recv.at[p, n, half], shifted(a3, e),
        )

    def middle_reduce(p, q, half):
        a1, a2, a3 = ORDERS[p]
        e = q[a2] + 2 * half
        return remote(
            S1.at[p, q[a2], half, q[a1]],
            R2.at[p, e - 1, q[a1]],
            r2_send.at[p, q[a1], e - 1], r2_recv.at[p, q[a1], e - 1], shifted(a2, e),
        )

    def each_heavy(n, act):
        r = parities(n)
        for p in range(3):
            for half in (0, 1):
                @pl.when(r[ORDERS[p][2]] + 2 * half != 0)
                def _(p=p, half=half):
                    act(p, half)

    def take_in(n):
        r = parities(n)
        each_heavy(n, lambda p, half: heavy_reduce(p, n, half).wait_recv())
        for p, (a1, a2, a3) in enumerate(ORDERS):
            @pl.when(r[a3] == 1)
            def _(p=p, a1=a1, a2=a2, a3=a3):
                rest = [r[i] for i in range(3) if i != a3]
                order = [i for i in range(3) if i != a3]
                own = part(GT, p, put(a3, 0, r), put(a3, 0, (ALL, ALL, ALL)))
                for i in (0, 1):
                    for j in (0, 1):
                        total = own[i, j].astype(jnp.float32)
                        for e in range(3):
                            total += R1[p, e, rest[0], rest[1], i, j].astype(jnp.float32)
                        total = total.astype(jnp.bfloat16)
                        hm, hl = (i, j) if order[0] == a2 else (j, i)
                        S1[p, r[a2], hm, r[a1], hl] = total
                for half in (0, 1):
                    @pl.when(r[a2] + 2 * half != 0)
                    def _(half=half):
                        middle_reduce(p, r, half).start()

    def body(n, _):
        r = parities(n)
        for p in range(3):
            for half in (0, 1):
                @pl.when(r[ORDERS[p][2]] + 2 * half != 0)
                def _(p=p, half=half):
                    heavy_gather(p, r, half).wait_recv()
        tile = T[r[0], r[1], r[2]].reshape(chunk, 3 * third)
        images = V[...]
        scores = lax.dot_general(
            tile, images, (((1,), (1,)), ((), ())), preferred_element_type=jnp.float32
        )
        row = lax.broadcasted_iota(jnp.int32, (chunk, 1), 0)
        at = [
            (me[i] + r[i] + 2 * ((row // (tdev << (2 - i))) % 2)) % 4 for i in range(3)
        ]
        names = (at[1] * 32 + at[2] * 8 + at[0] * 2 + core) * tdev + row % tdev
        match = names == IDR[...]
        t = slope * scores + shift
        t = jnp.where(match, -t, t)
        top = jnp.where(match, -scale, scale)
        weights = (top / (1.0 + jnp.exp2(t))).astype(jnp.bfloat16)
        GT[r[0], r[1], r[2]] = (
            jnp.dot(weights, images, preferred_element_type=jnp.float32)
            .astype(jnp.bfloat16)
            .reshape(2, 2, 2, tdev, 3 * third)
        )
        each_heavy(n, lambda p, half: heavy_reduce(p, n, half).start())
        GI[...] += lax.dot_general(
            weights, tile, (((0,), (0,)), ((), ())), preferred_element_type=jnp.float32
        )

        @pl.when(n >= lag)
        def _():
            take_in(n - lag)

        return 0

    lax.fori_loop(0, 8, body, 0)

    pieces = gi_recv.shape[0]
    step = rows // pieces
    swaps = [
        remote(
            GI.at[pl.ds(rows + i * step, step)], RB.at[pl.ds(i * step, step)],
            gi_send.at[i], gi_recv.at[i], sibling,
        )
        for i in range(pieces)
    ]
    for cp in swaps:
        cp.start()

    def last(n, _):
        take_in(n)
        return 0

    lax.fori_loop(8 - lag, 8, last, 0)

    outs = []

    def finish(i):
        swaps[i].wait_recv()
        at = pl.ds(i * step, step)
        RB[at, :] += GI[at, :]
        cp = pltpu.make_async_copy(RB.at[at], gi_out.at[at], out_sem.at[i])
        cp.start()
        outs.append(cp)

    for i in range(pieces // 2):
        finish(i)
    ends = []
    for p, (a1, a2, a3) in enumerate(ORDERS):
        for par in (0, 1):
            for e in (1, 2, 3):
                pltpu.make_async_copy(
                    R2.at[p, e - 1, par], R2.at[p, e - 1, par], r2_recv.at[p, par, e - 1]
                ).wait()
        for e in (2, 1, 3, 0):
            total = S1[p, 0, 0, e % 2, e // 2].astype(jnp.float32)
            for k in range(3):
                total += R2[p, k, e % 2, e // 2].astype(jnp.float32)
            if e:
                S2[p, e - 1] = total.astype(jnp.bfloat16)
                cp = remote(
                    S2.at[p, e - 1], R3.at[p, e - 1],
                    r3_send.at[p, e - 1], r3_recv.at[p, e - 1], shifted(a1, e),
                )
                cp.start()
                ends.append((p, e, cp))
            else:
                OUT[:, pl.ds(p * third, third)] = total
    for i in range(pieces // 2, pieces):
        finish(i)
    for p, e, cp in ends:
        cp.wait_recv()
    for p in range(3):
        cols = pl.ds(p * third, third)
        total = OUT[:, cols]
        for k in range(3):
            total += R3[p, k].astype(jnp.float32)
        OUT[:, cols] = total
    last_out = pltpu.make_async_copy(OUT, gt_out, out_sem.at[pieces])
    last_out.start()

    for cp in light + middle + [send_v, send_ids] + swaps + [cp for _, _, cp in ends]:
        cp.wait_send()
    for n in range(8):
        r = parities(n)
        for p in range(3):
            for half in (0, 1):
                if r[ORDERS[p][2]] + 2 * half:
                    heavy_gather(p, r, half).wait_send()
                    heavy_reduce(p, n, half).wait_send()
    for p, (a1, a2, a3) in enumerate(ORDERS):
        for low in (0, 1):
            for e in (1, 2, 3):
                q = put(a1, low, put(a2, e % 2, (0, 0, 0)))
                middle_reduce(p, q, e // 2).wait_send()
    for cp in outs + [last_out]:
        cp.wait()


def shards(images, texts, partners, scale, bias):
    rows, width = images.shape
    tdev = texts.shape[0]
    third = width // 3
    vmem = pltpu.VMEM
    sem = pltpu.SemaphoreType.DMA
    pieces = 4
    gathered = (2, 2, 2, 2, 2, 2, tdev, width)
    return pl.pallas_call(
        functools.partial(kernel, 1),
        out_shape=(
            jax.ShapeDtypeStruct((rows, width), jnp.float32),
            jax.ShapeDtypeStruct((tdev, width), jnp.float32),
        ),
        in_specs=[
            pl.BlockSpec(memory_space=pltpu.SMEM),
            pl.BlockSpec(memory_space=pltpu.SMEM),
            pl.BlockSpec(memory_space=pltpu.VMEM),
            pl.BlockSpec(memory_space=pl.ANY),
            pl.BlockSpec(memory_space=pl.ANY),
        ],
        out_specs=(pl.BlockSpec(memory_space=pl.ANY), pl.BlockSpec(memory_space=pl.ANY)),
        scratch_shapes=[
            vmem((2 * rows, width), jnp.bfloat16),
            vmem(gathered, jnp.bfloat16),
            vmem((2 * rows, width), jnp.float32),
            vmem(gathered, jnp.bfloat16),
            vmem((rows, width), jnp.float32),
            vmem((3, 3, 2, 2, 2, 2, tdev, third), jnp.bfloat16),
            vmem((3, 2, 2, 2, 2, tdev, third), jnp.bfloat16),
            vmem((3, 3, 2, 2, tdev, third), jnp.bfloat16),
            vmem((3, 3, tdev, third), jnp.bfloat16),
            vmem((3, 3, tdev, third), jnp.bfloat16),
            vmem((rows // 128, 128), jnp.int32),
            vmem((1, 2 * rows), jnp.int32),
            vmem((tdev, width), jnp.float32),
            sem((2,)), sem, sem, sem, sem, sem((pieces,)), sem((pieces,)), sem((pieces + 1,)),
            sem((3, 3)), sem((3, 3)), sem((3, 3)), sem((3, 3)), sem((3, 8, 2)), sem((3, 8, 2)),
            sem((3, 8, 2)), sem((3, 8, 2)), sem((3, 2, 3)), sem((3, 2, 3)), sem((3, 3)), sem((3, 3)),
        ],
        compiler_params=pltpu.CompilerParams(
            collective_id=0, has_side_effects=True, vmem_limit_bytes=60 * 2**20
        ),
        cost_estimate=pl.CostEstimate(
            flops=3 * 2 * 2 * rows * 64 * tdev * width, bytes_accessed=8 * rows * width, transcendentals=0
        ),
    )(
        scale.reshape(1, 1), bias.reshape(1, 1), partners.reshape(rows // 128, 128), images, texts
    )


def solution(mesh):
    return jax.shard_map(
        shards,
        mesh=mesh,
        in_specs=(P(AXES, None), P(AXES, None), P(AXES), P(), P()),
        out_specs=(P(AXES, None), P(AXES, None)),
        check_vma=False,
    )
```

```python
import functools

import jax
import jax.numpy as jnp
from jax import lax
from jax.experimental import pallas as pl
from jax.experimental.pallas import tpu as pltpu
from jax.sharding import PartitionSpec as P

AXES = ("wide", "blk")
MESH = pl.DeviceIdType.MESH
LOG2E = 1.4426950408889634
ORDERS = ((2, 1, 0), (1, 0, 2), (0, 2, 1))
ALL = slice(None)


def here():
    w, b = lax.axis_index("wide"), lax.axis_index("blk")
    return ((w % 2) * 2 + b // 2, w // 8, (w // 2) % 4), b % 2


def device(zyx, core):
    z, y, x = zyx
    return (y * 8 + x * 2 + z // 2, (z % 2) * 2 + core)


def kernel(
    lag,
    scale_ref, bias_ref, ids_ref, images_ref, texts_ref,
    gi_out, gt_out,
    V, T, W, GI, GT, RB, R1, S1, R2, S2, R3, IDS, IDR, OUT,
    in_sem, v_send, v_recv, id_send, id_recv, gi_send, gi_recv, out_sem,
    a1_send, a1_recv, a2_send, a2_recv, a3_send, a3_recv,
    r1_send, r1_recv, r2_send, r2_recv, r3_send, r3_recv,
):
    me, core = here()
    rows = images_ref.shape[0]
    third = texts_ref.shape[1] // 3
    tdev = texts_ref.shape[0]
    chunk = 8 * tdev
    sibling = device(me, 1 - core)

    def shifted(axis, by):
        pos = list(me)
        pos[axis] = (pos[axis] + by + 4) % 4
        return device(pos, core)

    def part(ref, p, par, half):
        return ref.at[(*par, *half, ALL, pl.ds(p * third, third))]

    def put(axis, offset, seq):
        seq = list(seq)
        seq[axis] = offset
        return tuple(seq)

    own_v = pltpu.make_async_copy(images_ref, V.at[pl.ds(0, rows)], in_sem.at[0])
    own_t = pltpu.make_async_copy(texts_ref, T.at[0, 0, 0, 0, 0, 0], in_sem.at[1])
    own_v.start()
    own_t.start()

    barrier = pltpu.get_barrier_semaphore()
    pl.semaphore_signal(barrier, inc=1, device_id=sibling, device_id_type=MESH)
    for axis in range(3):
        for e in (1, 2, 3):
            pl.semaphore_signal(barrier, inc=1, device_id=shifted(axis, e), device_id_type=MESH)
    pl.semaphore_wait(barrier, 10)

    def remote(src, dst, send, recv, to):
        return pltpu.make_async_remote_copy(
            src_ref=src, dst_ref=dst, send_sem=send, recv_sem=recv, device_id=to, device_id_type=MESH
        )

    def parities(n):
        m = 7 - n
        return (m // 4, (m // 2) % 2, m % 2)

    own_t.wait()
    zero = (0, 0, 0)

    def light_gather(p, e):
        a1 = ORDERS[p][0]
        return remote(
            part(T, p, zero, zero),
            part(T, p, put(a1, e % 2, zero), put(a1, e // 2, zero)),
            a1_send.at[p, e - 1], a1_recv.at[p, e - 1], shifted(a1, -e),
        )

    def middle_gather(p, low, e):
        a1, a2, a3 = ORDERS[p]
        par, half = put(a1, low, zero), put(a1, ALL, zero)
        return remote(
            part(T, p, par, half),
            part(T, p, put(a2, e % 2, par), put(a2, e // 2, half)),
            a2_send.at[p, low, e - 1], a2_recv.at[p, low, e - 1], shifted(a2, -e),
        )

    def heavy_gather(p, n, half):
        r = parities(n)
        a3 = ORDERS[p][2]
        both = put(a3, 0, (ALL, ALL, ALL))
        return remote(
            part(T, p, put(a3, 0, r), both),
            part(T, p, put(a3, 1, r), put(a3, half, both)),
            a3_send.at[p, n, half], a3_recv.at[p, n, half], shifted(a3, -1 - 2 * half),
        )

    def pass_on(p, n, half):
        r = parities(n)
        a3 = ORDERS[p][2]
        first = min(i for i in range(3) if i != a3)
        piece = put(first, half, (ALL, ALL, ALL))
        return remote(
            part(T, p, put(a3, 1, r), put(a3, half, piece)),
            part(T, p, put(a3, 0, r), put(a3, 1, piece)),
            a3_send.at[p, n, half], a3_recv.at[p, n, half], shifted(a3, 2 * half - 1),
        )

    for e in (1, 3, 2):
        for p in range(3):
            light_gather(p, e).start()
    send_v = remote(images_ref, V.at[pl.ds(rows, rows)], v_send, v_recv, sibling)
    send_v.start()
    send_ids = remote(ids_ref, IDS, id_send, id_recv, sibling)
    send_ids.start()
    for p in range(3):
        for e in (1, 3):
            light_gather(p, e).wait_recv()
        for e in (1, 3):
            middle_gather(p, 1, e).start()
    for p in range(3):
        light_gather(p, 2).wait_recv()
        for e in (1, 3):
            middle_gather(p, 0, e).start()
    for low in (1, 0):
        for p in range(3):
            middle_gather(p, low, 2).start()
    for n in range(8):
        r = parities(n)
        for p, (a1, a2, a3) in enumerate(ORDERS):
            if r[a3] == 1:
                for e in (1, 3) if r[a2] else (2,):
                    middle_gather(p, r[a1], e).wait_recv()
                for half in (0, 1):
                    heavy_gather(p, n, half).start()

    send_ids.wait_recv()
    for i in range(rows // 128):
        IDR[:, pl.ds(i * 128, 128)] = ids_ref[pl.ds(i, 1), :]
        IDR[:, pl.ds(rows + i * 128, 128)] = IDS[pl.ds(i, 1), :]
    own_v.wait()
    send_v.wait_recv()

    scale = scale_ref[0, 0]
    slope = -scale * LOG2E
    shift = -bias_ref[0, 0] * LOG2E

    def heavy_reduce(p, n, half):
        r = parities(n)
        a3 = ORDERS[p][2]
        e = r[a3] + 2 * half
        both = put(a3, half, (ALL, ALL, ALL))
        rest = [r[i] for i in range(3) if i != a3]
        return remote(
            part(GT, p, r, both),
            R1.at[p, e - 1, rest[0], rest[1]],
            r1_send.at[p, n, half], r1_recv.at[p, n, half], shifted(a3, e),
        )

    def middle_reduce(p, q, half):
        a1, a2, a3 = ORDERS[p]
        e = q[a2] + 2 * half
        return remote(
            S1.at[p, q[a2], half, q[a1]],
            R2.at[p, e - 1, q[a1]],
            r2_send.at[p, q[a1], e - 1], r2_recv.at[p, q[a1], e - 1], shifted(a2, e),
        )

    def each_heavy(n, act):
        r = parities(n)
        for p in range(3):
            for half in (0, 1):
                @pl.when(r[ORDERS[p][2]] + 2 * half != 0)
                def _(p=p, half=half):
                    act(p, half)

    def take_in(n):
        r = parities(n)
        each_heavy(n, lambda p, half: heavy_reduce(p, n, half).wait_recv())
        for p, (a1, a2, a3) in enumerate(ORDERS):
            @pl.when(r[a3] == 0)
            def _(p=p, a1=a1, a2=a2, a3=a3):
                rest = [r[i] for i in range(3) if i != a3]
                order = [i for i in range(3) if i != a3]
                own = part(GT, p, put(a3, 0, r), put(a3, 0, (ALL, ALL, ALL)))
                for i in (0, 1):
                    for j in (0, 1):
                        total = own[i, j].astype(jnp.float32)
                        for e in range(3):
                            total += R1[p, e, rest[0], rest[1], i, j].astype(jnp.float32)
                        total = total.astype(jnp.bfloat16)
                        hm, hl = (i, j) if order[0] == a2 else (j, i)
                        S1[p, r[a2], hm, r[a1], hl] = total
                for half in (0, 1):
                    @pl.when(r[a2] + 2 * half != 0)
                    def _(half=half):
                        middle_reduce(p, r, half).start()

    block = rows // 2

    def image_block(a, i, fresh):
        at = pl.ds(pl.multiple_of(i * block, block), block)
        terms = lax.dot_general(
            W[a, :, at], T[a].reshape(4 * chunk, 3 * third),
            (((0,), (0,)), ((), ())), preferred_element_type=jnp.float32,
        )
        GI[at, :] = terms if fresh else GI[at, :] + terms

    def body(n, _):
        r = parities(n)
        for p, (a1, a2, a3) in enumerate(ORDERS):
            @pl.when(r[a3] == 1)
            def _(p=p, a3=a3):
                for half in (0, 1):
                    heavy_gather(p, n, half).wait_recv()
                for half in (0, 1):
                    pass_on(p, n + (4 >> a3), half).start()

            @pl.when(r[a3] == 0)
            def _(p=p):
                for half in (0, 1):
                    pass_on(p, n, half).wait_recv()

        tile = T[r[0], r[1], r[2]].reshape(chunk, 3 * third)
        images = V[...]
        scores = lax.dot_general(
            tile, images, (((1,), (1,)), ((), ())), preferred_element_type=jnp.float32
        )
        row = lax.broadcasted_iota(jnp.int32, (chunk, 1), 0)
        at = [
            (me[i] + r[i] + 2 * ((row // (tdev << (2 - i))) % 2)) % 4 for i in range(3)
        ]
        names = (at[1] * 32 + at[2] * 8 + at[0] * 2 + core) * tdev + row % tdev
        match = names == IDR[...]
        t = slope * scores + shift
        t = jnp.where(match, -t, t)
        top = jnp.where(match, -scale, scale)
        weights = (top / (1.0 + jnp.exp2(t))).astype(jnp.bfloat16)
        GT[r[0], r[1], r[2]] = (
            jnp.dot(weights, images, preferred_element_type=jnp.float32)
            .astype(jnp.bfloat16)
            .reshape(2, 2, 2, tdev, 3 * third)
        )
        each_heavy(n, lambda p, half: heavy_reduce(p, n, half).start())
        W[r[0], pl.ds(pl.multiple_of((2 * r[1] + r[2]) * chunk, chunk), chunk), :] = weights

        @pl.when((n >= 3) & (n < 7))
        def _():
            image_block(1, n - 3, True)

        @pl.when(n >= lag)
        def _():
            take_in(n - lag)

        return 0

    lax.fori_loop(0, 8, body, 0)

    pieces = gi_recv.shape[0]
    step = rows // pieces
    swaps = [
        remote(
            GI.at[pl.ds(rows + i * step, step)], RB.at[pl.ds(i * step, step)],
            gi_send.at[i], gi_recv.at[i], sibling,
        )
        for i in range(pieces)
    ]

    def last(n, _):
        take_in(n)
        return 0

    lax.fori_loop(8 - lag, 7, last, 0)
    for i in range(pieces):
        image_block(0, 2 + i, False)
        swaps[i].start()
    take_in(7)
    image_block(0, 0, False)

    outs = []

    def finish(i):
        swaps[i].wait_recv()
        at = pl.ds(i * step, step)
        RB[at, :] += GI[at, :]
        cp = pltpu.make_async_copy(RB.at[at], gi_out.at[at], out_sem.at[i])
        cp.start()
        outs.append(cp)

    ends = []
    for p, (a1, a2, a3) in enumerate(ORDERS):
        for par in (0, 1):
            for e in (1, 2, 3):
                pltpu.make_async_copy(
                    R2.at[p, e - 1, par], R2.at[p, e - 1, par], r2_recv.at[p, par, e - 1]
                ).wait()
        for e in (2, 1, 3, 0):
            total = S1[p, 0, 0, e % 2, e // 2].astype(jnp.float32)
            for k in range(3):
                total += R2[p, k, e % 2, e // 2].astype(jnp.float32)
            if e:
                S2[p, e - 1] = total.astype(jnp.bfloat16)
                cp = remote(
                    S2.at[p, e - 1], R3.at[p, e - 1],
                    r3_send.at[p, e - 1], r3_recv.at[p, e - 1], shifted(a1, e),
                )
                cp.start()
                ends.append((p, e, cp))
            else:
                OUT[:, pl.ds(p * third, third)] = total
    image_block(0, 1, False)
    for i in range(pieces):
        finish(i)
    for p, e, cp in ends:
        cp.wait_recv()
    for p in range(3):
        cols = pl.ds(p * third, third)
        total = OUT[:, cols]
        for k in range(3):
            total += R3[p, k].astype(jnp.float32)
        OUT[:, cols] = total
    last_out = pltpu.make_async_copy(OUT, gt_out, out_sem.at[pieces])
    last_out.start()

    for cp in [send_v, send_ids] + swaps + [cp for _, _, cp in ends]:
        cp.wait_send()
    for p, (a1, a2, a3) in enumerate(ORDERS):
        for e in (1, 2, 3):
            light_gather(p, e).wait_send()
            for low in (0, 1):
                middle_gather(p, low, e).wait_send()
        for n in range(8):
            odd = parities(n)[a3]
            for half in (0, 1):
                (heavy_gather if odd else pass_on)(p, n, half).wait_send()
                if odd + 2 * half:
                    heavy_reduce(p, n, half).wait_send()
    for p, (a1, a2, a3) in enumerate(ORDERS):
        for low in (0, 1):
            for e in (1, 2, 3):
                q = put(a1, low, put(a2, e % 2, (0, 0, 0)))
                middle_reduce(p, q, e // 2).wait_send()
    for cp in outs + [last_out]:
        cp.wait()


def shards(images, texts, partners, scale, bias):
    rows, width = images.shape
    tdev = texts.shape[0]
    third = width // 3
    vmem = pltpu.VMEM
    sem = pltpu.SemaphoreType.DMA
    pieces = 2
    gathered = (2, 2, 2, 2, 2, 2, tdev, width)
    return pl.pallas_call(
        functools.partial(kernel, 2),
        out_shape=(
            jax.ShapeDtypeStruct((rows, width), jnp.float32),
            jax.ShapeDtypeStruct((tdev, width), jnp.float32),
        ),
        in_specs=[
            pl.BlockSpec(memory_space=pltpu.SMEM),
            pl.BlockSpec(memory_space=pltpu.SMEM),
            pl.BlockSpec(memory_space=pltpu.VMEM),
            pl.BlockSpec(memory_space=pl.ANY),
            pl.BlockSpec(memory_space=pl.ANY),
        ],
        out_specs=(pl.BlockSpec(memory_space=pl.ANY), pl.BlockSpec(memory_space=pl.ANY)),
        scratch_shapes=[
            vmem((2 * rows, width), jnp.bfloat16),
            vmem(gathered, jnp.bfloat16),
            vmem((2, 32 * tdev, 2 * rows), jnp.bfloat16),
            vmem((2 * rows, width), jnp.float32),
            vmem(gathered, jnp.bfloat16),
            vmem((rows, width), jnp.float32),
            vmem((3, 3, 2, 2, 2, 2, tdev, third), jnp.bfloat16),
            vmem((3, 2, 2, 2, 2, tdev, third), jnp.bfloat16),
            vmem((3, 3, 2, 2, tdev, third), jnp.bfloat16),
            vmem((3, 3, tdev, third), jnp.bfloat16),
            vmem((3, 3, tdev, third), jnp.bfloat16),
            vmem((rows // 128, 128), jnp.int32),
            vmem((1, 2 * rows), jnp.int32),
            vmem((tdev, width), jnp.float32),
            sem((2,)), sem, sem, sem, sem, sem((pieces,)), sem((pieces,)), sem((pieces + 1,)),
            sem((3, 3)), sem((3, 3)), sem((3, 2, 3)), sem((3, 2, 3)), sem((3, 8, 2)), sem((3, 8, 2)),
            sem((3, 8, 2)), sem((3, 8, 2)), sem((3, 2, 3)), sem((3, 2, 3)), sem((3, 3)), sem((3, 3)),
        ],
        compiler_params=pltpu.CompilerParams(
            collective_id=0, has_side_effects=True, vmem_limit_bytes=60 * 2**20
        ),
        cost_estimate=pl.CostEstimate(
            flops=3 * 2 * 2 * rows * 64 * tdev * width, bytes_accessed=8 * rows * width, transcendentals=0
        ),
    )(
        scale.reshape(1, 1), bias.reshape(1, 1), partners.reshape(rows // 128, 128), images, texts
    )


def solution(mesh):
    return jax.shard_map(
        shards,
        mesh=mesh,
        in_specs=(P(AXES, None), P(AXES, None), P(AXES), P(), P()),
        out_specs=(P(AXES, None), P(AXES, None)),
        check_vma=False,
    )
```

```python
import functools

import jax
import jax.numpy as jnp
from jax import lax
from jax.experimental import pallas as pl
from jax.experimental.pallas import tpu as pltpu
from jax.sharding import PartitionSpec as P

AXES = ("wide", "blk")
MESH = pl.DeviceIdType.MESH
LOG2E = 1.4426950408889634
ORDERS = ((2, 1, 0), (1, 0, 2), (0, 2, 1))
ALL = slice(None)
AHEAD = 2


def here():
    w, b = lax.axis_index("wide"), lax.axis_index("blk")
    return ((w % 2) * 2 + b // 2, w // 8, (w // 2) % 4), b % 2


def device(zyx, core):
    z, y, x = zyx
    return (y * 8 + x * 2 + z // 2, (z % 2) * 2 + core)


def kernel(
    lag,
    scale_ref, bias_ref, ids_ref, images_ref, texts_ref,
    gi_out, gt_out,
    V, T, W, GI, GT, RB, R1, S1, R2, S2, R3, IDS, IDR,
    in_sem, v_send, v_recv, id_send, id_recv, gi_send, gi_recv,
    a1_send, a1_recv, a2_send, a2_recv, a3_send, a3_recv,
    r1_send, r1_recv, r2_send, r2_recv, r3_send, r3_recv,
):
    me, core = here()
    rows = images_ref.shape[0]
    third = texts_ref.shape[1] // 3
    tdev = texts_ref.shape[0]
    chunk = 8 * tdev
    sibling = device(me, 1 - core)

    def shifted(axis, by):
        pos = list(me)
        pos[axis] = (pos[axis] + by + 4) % 4
        return device(pos, core)

    def part(ref, p, par, half):
        return ref.at[(*par, *half, ALL, pl.ds(p * third, third))]

    def put(axis, offset, seq):
        seq = list(seq)
        seq[axis] = offset
        return tuple(seq)

    own_v = pltpu.make_async_copy(images_ref, V.at[pl.ds(0, rows)], in_sem.at[0])
    own_t = pltpu.make_async_copy(texts_ref, T.at[0, 0, 0, 0, 0, 0], in_sem.at[1])
    own_v.start()
    own_t.start()

    barrier = pltpu.get_barrier_semaphore()
    pl.semaphore_signal(barrier, inc=1, device_id=sibling, device_id_type=MESH)
    for axis in range(3):
        for e in (1, 2, 3):
            pl.semaphore_signal(barrier, inc=1, device_id=shifted(axis, e), device_id_type=MESH)
    pl.semaphore_wait(barrier, 10)

    def remote(src, dst, send, recv, to):
        return pltpu.make_async_remote_copy(
            src_ref=src, dst_ref=dst, send_sem=send, recv_sem=recv, device_id=to, device_id_type=MESH
        )

    def parities(n):
        m = 7 - n
        return (m // 4, (m // 2) % 2, m % 2)

    own_t.wait()
    zero = (0, 0, 0)

    def light_gather(p, e):
        a1 = ORDERS[p][0]
        return remote(
            part(T, p, zero, zero),
            part(T, p, put(a1, e % 2, zero), put(a1, e // 2, zero)),
            a1_send.at[p, e - 1], a1_recv.at[p, e - 1], shifted(a1, -e),
        )

    def middle_gather(p, low, e):
        a1, a2, a3 = ORDERS[p]
        par, half = put(a1, low, zero), put(a1, ALL, zero)
        return remote(
            part(T, p, par, half),
            part(T, p, put(a2, e % 2, par), put(a2, e // 2, half)),
            a2_send.at[p, low, e - 1], a2_recv.at[p, low, e - 1], shifted(a2, -e),
        )

    def heavy_gather(p, n, half):
        r = parities(n)
        a3 = ORDERS[p][2]
        both = put(a3, 0, (ALL, ALL, ALL))
        return remote(
            part(T, p, put(a3, 0, r), both),
            part(T, p, put(a3, 1, r), put(a3, half, both)),
            a3_send.at[p, n, half], a3_recv.at[p, n, half], shifted(a3, -1 - 2 * half),
        )

    def pass_on(p, n, half):
        r = parities(n)
        a3 = ORDERS[p][2]
        first = min(i for i in range(3) if i != a3)
        piece = put(first, half, (ALL, ALL, ALL))
        return remote(
            part(T, p, put(a3, 1, r), put(a3, half, piece)),
            part(T, p, put(a3, 0, r), put(a3, 1, piece)),
            a3_send.at[p, n, half], a3_recv.at[p, n, half], shifted(a3, 2 * half - 1),
        )

    for e in (1, 3, 2):
        for p in range(3):
            light_gather(p, e).start()
    send_v = remote(images_ref, V.at[pl.ds(rows, rows)], v_send, v_recv, sibling)
    send_v.start()
    send_ids = remote(ids_ref, IDS, id_send, id_recv, sibling)
    send_ids.start()
    for p in range(3):
        for e in (1, 3):
            light_gather(p, e).wait_recv()
        for e in (1, 3):
            middle_gather(p, 1, e).start()
    for p in range(3):
        light_gather(p, 2).wait_recv()
        for e in (1, 3):
            middle_gather(p, 0, e).start()
    for low in (1, 0):
        for p in range(3):
            middle_gather(p, low, 2).start()
    waited = set()
    for n in range(AHEAD):
        r = parities(n)
        for p, (a1, a2, a3) in enumerate(ORDERS):
            if r[a3] == 1:
                for e in (1, 3) if r[a2] else (2,):
                    waited.add((p, r[a1], e))
                    middle_gather(p, r[a1], e).wait_recv()
                for half in (0, 1):
                    heavy_gather(p, n, half).start()
    for p in range(3):
        for low in (1, 0):
            for e in (1, 3, 2):
                if (p, low, e) not in waited:
                    middle_gather(p, low, e).wait_recv()

    send_ids.wait_recv()
    for i in range(rows // 128):
        IDR[:, pl.ds(i * 128, 128)] = ids_ref[pl.ds(i, 1), :]
        IDR[:, pl.ds(rows + i * 128, 128)] = IDS[pl.ds(i, 1), :]
    own_v.wait()
    send_v.wait_recv()

    scale = scale_ref[0, 0]
    slope = -scale * LOG2E
    shift = -bias_ref[0, 0] * LOG2E

    def heavy_reduce(p, n, half):
        r = parities(n)
        a3 = ORDERS[p][2]
        e = r[a3] + 2 * half
        both = put(a3, half, (ALL, ALL, ALL))
        rest = [r[i] for i in range(3) if i != a3]
        return remote(
            part(GT, p, r, both),
            R1.at[p, e - 1, rest[0], rest[1]],
            r1_send.at[p, n, half], r1_recv.at[p, n, half], shifted(a3, e),
        )

    def middle_reduce(p, q, half):
        a1, a2, a3 = ORDERS[p]
        e = q[a2] + 2 * half
        return remote(
            S1.at[p, q[a2], half, q[a1]],
            R2.at[p, e - 1, q[a1]],
            r2_send.at[p, q[a1], e - 1], r2_recv.at[p, q[a1], e - 1], shifted(a2, e),
        )

    def each_heavy(n, act):
        r = parities(n)
        for p in range(3):
            for half in (0, 1):
                @pl.when(r[ORDERS[p][2]] + 2 * half != 0)
                def _(p=p, half=half):
                    act(p, half)

    def take_in(n):
        r = parities(n)
        each_heavy(n, lambda p, half: heavy_reduce(p, n, half).wait_recv())
        for p, (a1, a2, a3) in enumerate(ORDERS):
            @pl.when(r[a3] == 0)
            def _(p=p, a1=a1, a2=a2, a3=a3):
                rest = [r[i] for i in range(3) if i != a3]
                order = [i for i in range(3) if i != a3]
                own = part(GT, p, put(a3, 0, r), put(a3, 0, (ALL, ALL, ALL)))
                for i in (0, 1):
                    for j in (0, 1):
                        total = own[i, j].astype(jnp.float32)
                        for e in range(3):
                            total += R1[p, e, rest[0], rest[1], i, j].astype(jnp.float32)
                        total = total.astype(jnp.bfloat16)
                        hm, hl = (i, j) if order[0] == a2 else (j, i)
                        S1[p, r[a2], hm, r[a1], hl] = total
                for half in (0, 1):
                    @pl.when(r[a2] + 2 * half != 0)
                    def _(half=half):
                        middle_reduce(p, r, half).start()

    pieces = gi_recv.shape[0]
    block = rows // pieces

    def image_block(i):
        at = pl.ds(i * block, block)
        GI[at, :] = lax.dot_general(
            W[:, at], T[...].reshape(8 * chunk, 3 * third),
            (((0,), (0,)), ((), ())), preferred_element_type=jnp.float32,
        )

    def body(n, _):
        r = parities(n)
        for p, (a1, a2, a3) in enumerate(ORDERS):
            @pl.when(r[a3] == 1)
            def _(p=p, a3=a3):
                for half in (0, 1):
                    heavy_gather(p, n, half).wait_recv()
                for half in (0, 1):
                    pass_on(p, n + (4 >> a3), half).start()

            @pl.when(r[a3] == 0)
            def _(p=p):
                for half in (0, 1):
                    pass_on(p, n, half).wait_recv()

        ahead = parities(n + AHEAD)
        for p, (a1, a2, a3) in enumerate(ORDERS):
            @pl.when((n + AHEAD < 8) & (ahead[a3] == 1))
            def _(p=p):
                for half in (0, 1):
                    heavy_gather(p, n + AHEAD, half).start()

        tile = T[r[0], r[1], r[2]].reshape(chunk, 3 * third)
        images = V[...]
        scores = lax.dot_general(
            tile, images, (((1,), (1,)), ((), ())), preferred_element_type=jnp.float32
        )
        row = lax.broadcasted_iota(jnp.int32, (chunk, 1), 0)
        at = [
            (me[i] + r[i] + 2 * ((row // (tdev << (2 - i))) % 2)) % 4 for i in range(3)
        ]
        names = (at[1] * 32 + at[2] * 8 + at[0] * 2 + core) * tdev + row % tdev
        match = names == IDR[...]
        t = slope * scores + shift
        t = jnp.where(match, -t, t)
        top = jnp.where(match, -scale, scale)
        weights = (top / (1.0 + jnp.exp2(t))).astype(jnp.bfloat16)
        GT[r[0], r[1], r[2]] = (
            jnp.dot(weights, images, preferred_element_type=jnp.float32)
            .astype(jnp.bfloat16)
            .reshape(2, 2, 2, tdev, 3 * third)
        )
        each_heavy(n, lambda p, half: heavy_reduce(p, n, half).start())
        W[pl.ds(pl.multiple_of((7 - n) * chunk, chunk), chunk), :] = weights

        @pl.when(n >= lag)
        def _():
            take_in(n - lag)

        return 0

    lax.fori_loop(0, 8, body, 0)

    step = block
    swaps = [
        remote(
            GI.at[pl.ds(rows + i * step, step)], RB.at[pl.ds(i * step, step)],
            gi_send.at[i], gi_recv.at[i], sibling,
        )
        for i in range(pieces)
    ]

    def finish(i):
        swaps[i].wait_recv()
        at = pl.ds(i * step, step)
        gi_out[at, :] = RB[at, :] + GI[at, :]

    for i in range(pieces):
        image_block(pieces + i)
        swaps[i].start()
        if i in (0, 2):
            take_in(6 + i // 2)
    for i in range(2):
        image_block(i)
    ends = []
    for p, (a1, a2, a3) in enumerate(ORDERS):
        for par in (0, 1):
            for e in (1, 2, 3):
                pltpu.make_async_copy(
                    R2.at[p, e - 1, par], R2.at[p, e - 1, par], r2_recv.at[p, par, e - 1]
                ).wait()
        for e in (2, 1, 3, 0):
            total = S1[p, 0, 0, e % 2, e // 2].astype(jnp.float32)
            for k in range(3):
                total += R2[p, k, e % 2, e // 2].astype(jnp.float32)
            if e:
                S2[p, e - 1] = total.astype(jnp.bfloat16)
                cp = remote(
                    S2.at[p, e - 1], R3.at[p, e - 1],
                    r3_send.at[p, e - 1], r3_recv.at[p, e - 1], shifted(a1, e),
                )
                cp.start()
                ends.append((p, e, cp))
            else:
                gt_out[:, pl.ds(p * third, third)] = total
    for i in range(2):
        finish(i)
    for i in range(2, pieces):
        image_block(i)
        finish(i)
    for p, e, cp in ends:
        cp.wait_recv()
    for p in range(3):
        cols = pl.ds(p * third, third)
        total = gt_out[:, cols]
        for k in range(3):
            total += R3[p, k].astype(jnp.float32)
        gt_out[:, cols] = total

    for cp in [send_v, send_ids] + swaps + [cp for _, _, cp in ends]:
        cp.wait_send()
    for p, (a1, a2, a3) in enumerate(ORDERS):
        for e in (1, 2, 3):
            light_gather(p, e).wait_send()
            for low in (0, 1):
                middle_gather(p, low, e).wait_send()
        for n in range(8):
            odd = parities(n)[a3]
            for half in (0, 1):
                (heavy_gather if odd else pass_on)(p, n, half).wait_send()
                if odd + 2 * half:
                    heavy_reduce(p, n, half).wait_send()
    for p, (a1, a2, a3) in enumerate(ORDERS):
        for low in (0, 1):
            for e in (1, 2, 3):
                q = put(a1, low, put(a2, e % 2, (0, 0, 0)))
                middle_reduce(p, q, e // 2).wait_send()


def shards(images, texts, partners, scale, bias):
    rows, width = images.shape
    tdev = texts.shape[0]
    third = width // 3
    vmem = pltpu.VMEM
    sem = pltpu.SemaphoreType.DMA
    pieces = 4
    gathered = (2, 2, 2, 2, 2, 2, tdev, width)
    return pl.pallas_call(
        functools.partial(kernel, 2),
        out_shape=(
            pltpu.VMEM((rows, width), jnp.float32),
            pltpu.VMEM((tdev, width), jnp.float32),
        ),
        in_specs=[
            pl.BlockSpec(memory_space=pltpu.SMEM),
            pl.BlockSpec(memory_space=pltpu.SMEM),
            pl.BlockSpec(memory_space=pltpu.VMEM),
            pl.BlockSpec(memory_space=pltpu.HBM),
            pl.BlockSpec(memory_space=pltpu.HBM),
        ],
        out_specs=(pl.BlockSpec(memory_space=pltpu.VMEM), pl.BlockSpec(memory_space=pltpu.VMEM)),
        scratch_shapes=[
            vmem((2 * rows, width), jnp.bfloat16),
            vmem(gathered, jnp.bfloat16),
            vmem((64 * tdev, 2 * rows), jnp.bfloat16),
            vmem((2 * rows, width), jnp.float32),
            vmem(gathered, jnp.bfloat16),
            vmem((rows, width), jnp.float32),
            vmem((3, 3, 2, 2, 2, 2, tdev, third), jnp.bfloat16),
            vmem((3, 2, 2, 2, 2, tdev, third), jnp.bfloat16),
            vmem((3, 3, 2, 2, tdev, third), jnp.bfloat16),
            vmem((3, 3, tdev, third), jnp.bfloat16),
            vmem((3, 3, tdev, third), jnp.bfloat16),
            vmem((rows // 128, 128), jnp.int32),
            vmem((1, 2 * rows), jnp.int32),
            sem((2,)), sem, sem, sem, sem, sem((pieces,)), sem((pieces,)),
            sem((3, 3)), sem((3, 3)), sem((3, 2, 3)), sem((3, 2, 3)), sem((3, 8, 2)), sem((3, 8, 2)),
            sem((3, 8, 2)), sem((3, 8, 2)), sem((3, 2, 3)), sem((3, 2, 3)), sem((3, 3)), sem((3, 3)),
        ],
        compiler_params=pltpu.CompilerParams(
            collective_id=0, has_side_effects=True, vmem_limit_bytes=52 * 2**20
        ),
        cost_estimate=pl.CostEstimate(
            flops=3 * 2 * 2 * rows * 64 * tdev * width, bytes_accessed=8 * rows * width, transcendentals=0
        ),
    )(
        scale.reshape(1, 1), bias.reshape(1, 1), partners.reshape(rows // 128, 128), images, texts
    )


def solution(mesh):
    return jax.shard_map(
        shards,
        mesh=mesh,
        in_specs=(P(AXES, None), P(AXES, None), P(AXES), P(), P()),
        out_specs=(P(AXES, None), P(AXES, None)),
        check_vma=False,
    )
```

```python
import functools

import jax
import jax.numpy as jnp
from jax import lax
from jax.experimental import pallas as pl
from jax.experimental.pallas import tpu as pltpu
from jax.sharding import PartitionSpec as P

AXES = ("wide", "blk")
MESH = pl.DeviceIdType.MESH
LOG2E = 1.4426950408889634
ORDERS = ((2, 1, 0), (1, 0, 2), (0, 2, 1))
ALL = slice(None)
AHEAD = 2


def here():
    w, b = lax.axis_index("wide"), lax.axis_index("blk")
    return ((w % 2) * 2 + b // 2, w // 8, (w // 2) % 4), b % 2


def device(zyx, core):
    z, y, x = zyx
    return (y * 8 + x * 2 + z // 2, (z % 2) * 2 + core)


def kernel(
    lag,
    scale_ref, bias_ref, ids_ref, images_ref, texts_ref,
    gi_out, gt_out,
    V, T, W, GI, GT, RB, R1, S1, R2, S2, R3, IDS, IDR,
    in_sem, v_send, v_recv, id_send, id_recv, gi_send, gi_recv,
    a1_send, a1_recv, a2_send, a2_recv, a3_send, a3_recv,
    r1_send, r1_recv, r2_send, r2_recv, r3_send, r3_recv,
):
    me, core = here()
    rows = images_ref.shape[0]
    third = texts_ref.shape[1] // 3
    tdev = texts_ref.shape[0]
    chunk = 8 * tdev
    sibling = device(me, 1 - core)

    def shifted(axis, by):
        pos = list(me)
        pos[axis] = (pos[axis] + by + 4) % 4
        return device(pos, core)

    def part(ref, p, par, half):
        return ref.at[(*par, *half, ALL, pl.ds(p * third, third))]

    def put(axis, offset, seq):
        seq = list(seq)
        seq[axis] = offset
        return tuple(seq)

    own_v = pltpu.make_async_copy(images_ref, V.at[pl.ds(0, rows)], in_sem.at[0])
    own_t = pltpu.make_async_copy(texts_ref, T.at[0, 0, 0, 0, 0, 0], in_sem.at[1])
    own_v.start()
    own_t.start()

    barrier = pltpu.get_barrier_semaphore()
    pl.semaphore_signal(barrier, inc=1, device_id=sibling, device_id_type=MESH)
    for axis in range(3):
        for e in (1, 2, 3):
            pl.semaphore_signal(barrier, inc=1, device_id=shifted(axis, e), device_id_type=MESH)
    pl.semaphore_wait(barrier, 10)

    def remote(src, dst, send, recv, to):
        return pltpu.make_async_remote_copy(
            src_ref=src, dst_ref=dst, send_sem=send, recv_sem=recv, device_id=to, device_id_type=MESH
        )

    def parities(n):
        m = 7 - n
        return (m // 4, (m // 2) % 2, m % 2)

    own_t.wait()
    zero = (0, 0, 0)

    def light_gather(p, e):
        a1 = ORDERS[p][0]
        return remote(
            part(T, p, zero, zero),
            part(T, p, put(a1, e % 2, zero), put(a1, e // 2, zero)),
            a1_send.at[p, e - 1], a1_recv.at[p, e - 1], shifted(a1, -e),
        )

    def middle_gather(p, low, e):
        a1, a2, a3 = ORDERS[p]
        par, half = put(a1, low, zero), put(a1, ALL, zero)
        return remote(
            part(T, p, par, half),
            part(T, p, put(a2, e % 2, par), put(a2, e // 2, half)),
            a2_send.at[p, low, e - 1], a2_recv.at[p, low, e - 1], shifted(a2, -e),
        )

    def heavy_gather(p, n, half):
        r = parities(n)
        a3 = ORDERS[p][2]
        both = put(a3, 0, (ALL, ALL, ALL))
        return remote(
            part(T, p, put(a3, 0, r), both),
            part(T, p, put(a3, 1, r), put(a3, half, both)),
            a3_send.at[p, n, half], a3_recv.at[p, n, half], shifted(a3, -1 - 2 * half),
        )

    def pass_on(p, n, half):
        r = parities(n)
        a3 = ORDERS[p][2]
        first = min(i for i in range(3) if i != a3)
        piece = put(first, half, (ALL, ALL, ALL))
        return remote(
            part(T, p, put(a3, 1, r), put(a3, half, piece)),
            part(T, p, put(a3, 0, r), put(a3, 1, piece)),
            a3_send.at[p, n, half], a3_recv.at[p, n, half], shifted(a3, 2 * half - 1),
        )

    for e in (1, 3, 2):
        for p in range(3):
            light_gather(p, e).start()
    send_v = remote(images_ref, V.at[pl.ds(rows, rows)], v_send, v_recv, sibling)
    send_v.start()
    send_ids = remote(ids_ref, IDS, id_send, id_recv, sibling)
    send_ids.start()
    for p in range(3):
        for e in (1, 3):
            light_gather(p, e).wait_recv()
        for e in (1, 3):
            middle_gather(p, 1, e).start()
    for p in range(3):
        light_gather(p, 2).wait_recv()
        for e in (1, 3):
            middle_gather(p, 0, e).start()
    for low in (1, 0):
        for p in range(3):
            middle_gather(p, low, 2).start()
    waited = set()
    for n in range(AHEAD):
        r = parities(n)
        for p, (a1, a2, a3) in enumerate(ORDERS):
            if r[a3] == 1:
                for e in (1, 3) if r[a2] else (2,):
                    waited.add((p, r[a1], e))
                    middle_gather(p, r[a1], e).wait_recv()
                for half in (0, 1):
                    heavy_gather(p, n, half).start()
    for p in range(3):
        for low in (1, 0):
            for e in (1, 3, 2):
                if (p, low, e) not in waited:
                    middle_gather(p, low, e).wait_recv()

    send_ids.wait_recv()
    for i in range(rows // 128):
        IDR[:, pl.ds(i * 128, 128)] = ids_ref[pl.ds(i, 1), :]
        IDR[:, pl.ds(rows + i * 128, 128)] = IDS[pl.ds(i, 1), :]
    own_v.wait()
    send_v.wait_recv()

    scale = scale_ref[0, 0]
    slope = -scale * LOG2E
    shift = -bias_ref[0, 0] * LOG2E

    def heavy_reduce(p, n, half):
        r = parities(n)
        a3 = ORDERS[p][2]
        e = r[a3] + 2 * half
        both = put(a3, half, (ALL, ALL, ALL))
        rest = [r[i] for i in range(3) if i != a3]
        return remote(
            part(GT, p, r, both),
            R1.at[p, e - 1, rest[0], rest[1]],
            r1_send.at[p, n, half], r1_recv.at[p, n, half], shifted(a3, e),
        )

    def middle_reduce(p, q, half):
        a1, a2, a3 = ORDERS[p]
        e = q[a2] + 2 * half
        return remote(
            S1.at[p, q[a2], half, q[a1]],
            R2.at[p, e - 1, q[a1]],
            r2_send.at[p, q[a1], e - 1], r2_recv.at[p, q[a1], e - 1], shifted(a2, e),
        )

    def each_heavy(n, act):
        r = parities(n)
        for p in range(3):
            for half in (0, 1):
                @pl.when(r[ORDERS[p][2]] + 2 * half != 0)
                def _(p=p, half=half):
                    act(p, half)

    def take_in(n):
        r = parities(n)
        each_heavy(n, lambda p, half: heavy_reduce(p, n, half).wait_recv())
        for p, (a1, a2, a3) in enumerate(ORDERS):
            @pl.when(r[a3] == 0)
            def _(p=p, a1=a1, a2=a2, a3=a3):
                rest = [r[i] for i in range(3) if i != a3]
                order = [i for i in range(3) if i != a3]
                own = part(GT, p, put(a3, 0, r), put(a3, 0, (ALL, ALL, ALL)))
                for i in (0, 1):
                    for j in (0, 1):
                        total = own[i, j].astype(jnp.float32)
                        for e in range(3):
                            total += R1[p, e, rest[0], rest[1], i, j].astype(jnp.float32)
                        total = total.astype(jnp.bfloat16)
                        hm, hl = (i, j) if order[0] == a2 else (j, i)
                        S1[p, r[a2], hm, r[a1], hl] = total
                for half in (0, 1):
                    @pl.when(r[a2] + 2 * half != 0)
                    def _(half=half):
                        middle_reduce(p, r, half).start()

    pieces = gi_recv.shape[0]
    block = rows // pieces

    def image_block(i):
        at = pl.ds(i * block, block)
        GI[at, :] = lax.dot_general(
            W[:, at], T[...].reshape(8 * chunk, 3 * third),
            (((0,), (0,)), ((), ())), preferred_element_type=jnp.float32,
        )

    def body(n, _):
        r = parities(n)
        for p, (a1, a2, a3) in enumerate(ORDERS):
            @pl.when(r[a3] == 1)
            def _(p=p, a3=a3):
                for half in (0, 1):
                    heavy_gather(p, n, half).wait_recv()
                for half in (0, 1):
                    pass_on(p, n + (4 >> a3), half).start()

            @pl.when(r[a3] == 0)
            def _(p=p):
                for half in (0, 1):
                    pass_on(p, n, half).wait_recv()

        ahead = parities(n + AHEAD)
        for p, (a1, a2, a3) in enumerate(ORDERS):
            @pl.when((n + AHEAD < 8) & (ahead[a3] == 1))
            def _(p=p):
                for half in (0, 1):
                    heavy_gather(p, n + AHEAD, half).start()

        tile = T[r[0], r[1], r[2]].reshape(chunk, 3 * third)
        images = V[...]
        scores = lax.dot_general(
            tile, images, (((1,), (1,)), ((), ())), preferred_element_type=jnp.float32
        )
        row = lax.broadcasted_iota(jnp.int32, (chunk, 1), 0)
        at = [
            (me[i] + r[i] + 2 * ((row // (tdev << (2 - i))) % 2)) % 4 for i in range(3)
        ]
        names = (at[1] * 32 + at[2] * 8 + at[0] * 2 + core) * tdev + row % tdev
        match = names == IDR[...]
        t = slope * scores + shift
        t = jnp.where(match, -t, t)
        top = jnp.where(match, -scale, scale)
        weights = (top / (1.0 + jnp.exp2(t))).astype(jnp.bfloat16)
        GT[r[0], r[1], r[2]] = (
            jnp.dot(weights, images, preferred_element_type=jnp.float32)
            .astype(jnp.bfloat16)
            .reshape(2, 2, 2, tdev, 3 * third)
        )
        each_heavy(n, lambda p, half: heavy_reduce(p, n, half).start())
        W[pl.ds(pl.multiple_of((7 - n) * chunk, chunk), chunk), :] = weights

        @pl.when(n >= lag)
        def _():
            take_in(n - lag)

        return 0

    lax.fori_loop(0, 8, body, 0)

    step = block
    swaps = [
        remote(
            GI.at[pl.ds(rows + i * step, step)], RB.at[pl.ds(i * step, step)],
            gi_send.at[i], gi_recv.at[i], sibling,
        )
        for i in range(pieces)
    ]

    def finish(i):
        swaps[i].wait_recv()
        at = pl.ds(i * step, step)
        gi_out[at, :] = RB[at, :] + GI[at, :]

    for i in range(pieces):
        image_block(pieces + i)
        swaps[i].start()
        if i < 3:
            take_in(5 + i)
    ends = []

    def light_reduce(par):
        for p, (a1, a2, a3) in enumerate(ORDERS):
            for e in (1, 2, 3):
                pltpu.make_async_copy(
                    R2.at[p, e - 1, par], R2.at[p, e - 1, par], r2_recv.at[p, par, e - 1]
                ).wait()
            for e in (1, 3) if par else (2, 0):
                total = S1[p, 0, 0, e % 2, e // 2].astype(jnp.float32)
                for k in range(3):
                    total += R2[p, k, e % 2, e // 2].astype(jnp.float32)
                if e:
                    S2[p, e - 1] = total.astype(jnp.bfloat16)
                    cp = remote(
                        S2.at[p, e - 1], R3.at[p, e - 1],
                        r3_send.at[p, e - 1], r3_recv.at[p, e - 1], shifted(a1, e),
                    )
                    cp.start()
                    ends.append((p, e, cp))
                else:
                    gt_out[:, pl.ds(p * third, third)] = total

    image_block(0)
    light_reduce(1)
    image_block(1)
    light_reduce(0)
    for i in range(2):
        finish(i)
    for i in range(2, pieces):
        image_block(i)
        finish(i)
    for p, e, cp in ends:
        cp.wait_recv()
    for p in range(3):
        cols = pl.ds(p * third, third)
        total = gt_out[:, cols]
        for k in range(3):
            total += R3[p, k].astype(jnp.float32)
        gt_out[:, cols] = total

    for cp in [send_v, send_ids] + swaps + [cp for _, _, cp in ends]:
        cp.wait_send()
    for p, (a1, a2, a3) in enumerate(ORDERS):
        for e in (1, 2, 3):
            light_gather(p, e).wait_send()
            for low in (0, 1):
                middle_gather(p, low, e).wait_send()
        for n in range(8):
            odd = parities(n)[a3]
            for half in (0, 1):
                (heavy_gather if odd else pass_on)(p, n, half).wait_send()
                if odd + 2 * half:
                    heavy_reduce(p, n, half).wait_send()
    for p, (a1, a2, a3) in enumerate(ORDERS):
        for low in (0, 1):
            for e in (1, 2, 3):
                q = put(a1, low, put(a2, e % 2, (0, 0, 0)))
                middle_reduce(p, q, e // 2).wait_send()


def shards(images, texts, partners, scale, bias):
    rows, width = images.shape
    tdev = texts.shape[0]
    third = width // 3
    vmem = pltpu.VMEM
    sem = pltpu.SemaphoreType.DMA
    pieces = 4
    gathered = (2, 2, 2, 2, 2, 2, tdev, width)
    return pl.pallas_call(
        functools.partial(kernel, 3),
        out_shape=(
            pltpu.VMEM((rows, width), jnp.float32),
            pltpu.VMEM((tdev, width), jnp.float32),
        ),
        in_specs=[
            pl.BlockSpec(memory_space=pltpu.SMEM),
            pl.BlockSpec(memory_space=pltpu.SMEM),
            pl.BlockSpec(memory_space=pltpu.VMEM),
            pl.BlockSpec(memory_space=pltpu.HBM),
            pl.BlockSpec(memory_space=pltpu.HBM),
        ],
        out_specs=(pl.BlockSpec(memory_space=pltpu.VMEM), pl.BlockSpec(memory_space=pltpu.VMEM)),
        scratch_shapes=[
            vmem((2 * rows, width), jnp.bfloat16),
            vmem(gathered, jnp.bfloat16),
            vmem((64 * tdev, 2 * rows), jnp.bfloat16),
            vmem((2 * rows, width), jnp.float32),
            vmem(gathered, jnp.bfloat16),
            vmem((rows, width), jnp.float32),
            vmem((3, 3, 2, 2, 2, 2, tdev, third), jnp.bfloat16),
            vmem((3, 2, 2, 2, 2, tdev, third), jnp.bfloat16),
            vmem((3, 3, 2, 2, tdev, third), jnp.bfloat16),
            vmem((3, 3, tdev, third), jnp.bfloat16),
            vmem((3, 3, tdev, third), jnp.bfloat16),
            vmem((rows // 128, 128), jnp.int32),
            vmem((1, 2 * rows), jnp.int32),
            sem((2,)), sem, sem, sem, sem, sem((pieces,)), sem((pieces,)),
            sem((3, 3)), sem((3, 3)), sem((3, 2, 3)), sem((3, 2, 3)), sem((3, 8, 2)), sem((3, 8, 2)),
            sem((3, 8, 2)), sem((3, 8, 2)), sem((3, 2, 3)), sem((3, 2, 3)), sem((3, 3)), sem((3, 3)),
        ],
        compiler_params=pltpu.CompilerParams(
            collective_id=0, has_side_effects=True, vmem_limit_bytes=52 * 2**20
        ),
        cost_estimate=pl.CostEstimate(
            flops=3 * 2 * 2 * rows * 64 * tdev * width, bytes_accessed=8 * rows * width, transcendentals=0
        ),
    )(
        scale.reshape(1, 1), bias.reshape(1, 1), partners.reshape(rows // 128, 128), images, texts
    )


def solution(mesh):
    return jax.shard_map(
        shards,
        mesh=mesh,
        in_specs=(P(AXES, None), P(AXES, None), P(AXES), P(), P()),
        out_specs=(P(AXES, None), P(AXES, None)),
        check_vma=False,
    )
```

```python
import functools

import jax
import jax.numpy as jnp
from jax import lax
from jax.experimental import pallas as pl
from jax.experimental.pallas import tpu as pltpu
from jax.sharding import PartitionSpec as P

AXES = ("wide", "blk")
MESH = pl.DeviceIdType.MESH
LOG2E = 1.4426950408889634
ORDERS = ((2, 1, 0), (1, 0, 2), (0, 2, 1))
ALL = slice(None)
AHEAD = 2


def here():
    w, b = lax.axis_index("wide"), lax.axis_index("blk")
    return ((w % 2) * 2 + b // 2, w // 8, (w // 2) % 4), b % 2


def device(zyx, core):
    z, y, x = zyx
    return (y * 8 + x * 2 + z // 2, (z % 2) * 2 + core)


def kernel(
    lag,
    scale_ref, bias_ref, ids_ref, images_ref, texts_ref,
    gi_out, gt_out,
    V, T, W, GI, GT, RB, R1, S1, R2, S2, R3, IDS, IDR,
    in_sem, v_send, v_recv, id_send, id_recv, gi_send, gi_recv,
    a1_send, a1_recv, a2_send, a2_recv, a3_send, a3_recv,
    r1_send, r1_recv, r2_send, r2_recv, r3_send, r3_recv,
):
    me, core = here()
    rows = images_ref.shape[0]
    third = texts_ref.shape[1] // 3
    tdev = texts_ref.shape[0]
    chunk = 8 * tdev
    sibling = device(me, 1 - core)

    def shifted(axis, by):
        pos = list(me)
        pos[axis] = (pos[axis] + by + 4) % 4
        return device(pos, core)

    def part(ref, p, par, half):
        return ref.at[(*par, *half, ALL, pl.ds(p * third, third))]

    def put(axis, offset, seq):
        seq = list(seq)
        seq[axis] = offset
        return tuple(seq)

    own_v = pltpu.make_async_copy(images_ref, V.at[pl.ds(0, rows)], in_sem.at[0])
    own_t = pltpu.make_async_copy(texts_ref, T.at[0, 0, 0, 0, 0, 0], in_sem.at[1])
    own_v.start()
    own_t.start()

    barrier = pltpu.get_barrier_semaphore()
    pl.semaphore_signal(barrier, inc=1, device_id=sibling, device_id_type=MESH)
    for axis in range(3):
        for e in (1, 2, 3):
            pl.semaphore_signal(barrier, inc=1, device_id=shifted(axis, e), device_id_type=MESH)
    pl.semaphore_wait(barrier, 10)

    def remote(src, dst, send, recv, to):
        return pltpu.make_async_remote_copy(
            src_ref=src, dst_ref=dst, send_sem=send, recv_sem=recv, device_id=to, device_id_type=MESH
        )

    def parities(n):
        m = 7 - n
        return (m // 4, (m // 2) % 2, m % 2)

    own_t.wait()
    zero = (0, 0, 0)

    def light_gather(p, e):
        a1 = ORDERS[p][0]
        return remote(
            part(T, p, zero, zero),
            part(T, p, put(a1, e % 2, zero), put(a1, e // 2, zero)),
            a1_send.at[p, e - 1], a1_recv.at[p, e - 1], shifted(a1, -e),
        )

    def middle_gather(p, low, e):
        a1, a2, a3 = ORDERS[p]
        par, half = put(a1, low, zero), put(a1, ALL, zero)
        return remote(
            part(T, p, par, half),
            part(T, p, put(a2, e % 2, par), put(a2, e // 2, half)),
            a2_send.at[p, low, e - 1], a2_recv.at[p, low, e - 1], shifted(a2, -e),
        )

    def heavy_gather(p, n, half):
        r = parities(n)
        a3 = ORDERS[p][2]
        both = put(a3, 0, (ALL, ALL, ALL))
        return remote(
            part(T, p, put(a3, 0, r), both),
            part(T, p, put(a3, 1, r), put(a3, half, both)),
            a3_send.at[p, n, half], a3_recv.at[p, n, half], shifted(a3, -1 - 2 * half),
        )

    def pass_on(p, n, half):
        r = parities(n)
        a3 = ORDERS[p][2]
        first = min(i for i in range(3) if i != a3)
        piece = put(first, half, (ALL, ALL, ALL))
        return remote(
            part(T, p, put(a3, 1, r), put(a3, half, piece)),
            part(T, p, put(a3, 0, r), put(a3, 1, piece)),
            a3_send.at[p, n, half], a3_recv.at[p, n, half], shifted(a3, 2 * half - 1),
        )

    for e in (1, 3, 2):
        for p in range(3):
            light_gather(p, e).start()
    send_v = remote(images_ref, V.at[pl.ds(rows, rows)], v_send, v_recv, sibling)
    send_v.start()
    send_ids = remote(ids_ref, IDS, id_send, id_recv, sibling)
    send_ids.start()
    for p in range(3):
        for e in (1, 3):
            light_gather(p, e).wait_recv()
        for e in (1, 3):
            middle_gather(p, 1, e).start()
    for p in range(3):
        light_gather(p, 2).wait_recv()
        for e in (1, 3):
            middle_gather(p, 0, e).start()
    for low in (1, 0):
        for p in range(3):
            middle_gather(p, low, 2).start()
    waited = set()
    for n in range(AHEAD):
        r = parities(n)
        for p, (a1, a2, a3) in enumerate(ORDERS):
            if r[a3] == 1:
                for e in (1, 3) if r[a2] else (2,):
                    waited.add((p, r[a1], e))
                    middle_gather(p, r[a1], e).wait_recv()
                for half in (0, 1):
                    heavy_gather(p, n, half).start()
    for p in range(3):
        for low in (1, 0):
            for e in (1, 3, 2):
                if (p, low, e) not in waited:
                    middle_gather(p, low, e).wait_recv()

    send_ids.wait_recv()
    for i in range(rows // 128):
        IDR[:, pl.ds(i * 128, 128)] = ids_ref[pl.ds(i, 1), :]
        IDR[:, pl.ds(rows + i * 128, 128)] = IDS[pl.ds(i, 1), :]
    own_v.wait()
    send_v.wait_recv()

    scale = scale_ref[0, 0]
    slope = -scale * LOG2E
    shift = -bias_ref[0, 0] * LOG2E

    def heavy_reduce(p, n, half):
        r = parities(n)
        a3 = ORDERS[p][2]
        e = r[a3] + 2 * half
        both = put(a3, half, (ALL, ALL, ALL))
        rest = [r[i] for i in range(3) if i != a3]
        return remote(
            part(GT, p, r, both),
            R1.at[p, e - 1, rest[0], rest[1]],
            r1_send.at[p, n, half], r1_recv.at[p, n, half], shifted(a3, e),
        )

    def middle_reduce(p, q, half):
        a1, a2, a3 = ORDERS[p]
        e = q[a2] + 2 * half
        return remote(
            S1.at[p, q[a2], half, q[a1]],
            R2.at[p, e - 1, q[a1]],
            r2_send.at[p, q[a1], e - 1], r2_recv.at[p, q[a1], e - 1], shifted(a2, e),
        )

    def each_heavy(n, act):
        r = parities(n)
        for p in range(3):
            for half in (0, 1):
                @pl.when(r[ORDERS[p][2]] + 2 * half != 0)
                def _(p=p, half=half):
                    act(p, half)

    def take_in(n):
        r = parities(n)
        each_heavy(n, lambda p, half: heavy_reduce(p, n, half).wait_recv())
        for p, (a1, a2, a3) in enumerate(ORDERS):
            @pl.when(r[a3] == 0)
            def _(p=p, a1=a1, a2=a2, a3=a3):
                rest = [r[i] for i in range(3) if i != a3]
                order = [i for i in range(3) if i != a3]
                own = part(GT, p, put(a3, 0, r), put(a3, 0, (ALL, ALL, ALL)))
                for i in (0, 1):
                    for j in (0, 1):
                        total = own[i, j].astype(jnp.float32)
                        for e in range(3):
                            total += R1[p, e, rest[0], rest[1], i, j].astype(jnp.float32)
                        total = total.astype(jnp.bfloat16)
                        hm, hl = (i, j) if order[0] == a2 else (j, i)
                        S1[p, r[a2], hm, r[a1], hl] = total
                for half in (0, 1):
                    @pl.when(r[a2] + 2 * half != 0)
                    def _(half=half):
                        middle_reduce(p, r, half).start()

    pieces = gi_recv.shape[0]
    block = rows // pieces

    def image_block(i, count=1):
        at = pl.ds(i * block, count * block)
        GI[at, :] = lax.dot_general(
            W[:, at], T[...].reshape(8 * chunk, 3 * third),
            (((0,), (0,)), ((), ())), preferred_element_type=jnp.float32,
        )

    def body(n, _):
        r = parities(n)
        for p, (a1, a2, a3) in enumerate(ORDERS):
            @pl.when(r[a3] == 1)
            def _(p=p, a3=a3):
                for half in (0, 1):
                    heavy_gather(p, n, half).wait_recv()
                for half in (0, 1):
                    pass_on(p, n + (4 >> a3), half).start()

            @pl.when(r[a3] == 0)
            def _(p=p):
                for half in (0, 1):
                    pass_on(p, n, half).wait_recv()

        ahead = parities(n + AHEAD)
        for p, (a1, a2, a3) in enumerate(ORDERS):
            @pl.when((n + AHEAD < 8) & (ahead[a3] == 1))
            def _(p=p):
                for half in (0, 1):
                    heavy_gather(p, n + AHEAD, half).start()

        tile = T[r[0], r[1], r[2]].reshape(chunk, 3 * third)
        images = V[...]
        scores = lax.dot_general(
            tile, images, (((1,), (1,)), ((), ())), preferred_element_type=jnp.float32
        )
        row = lax.broadcasted_iota(jnp.int32, (chunk, 1), 0)
        at = [
            (me[i] + r[i] + 2 * ((row // (tdev << (2 - i))) % 2)) % 4 for i in range(3)
        ]
        names = (at[1] * 32 + at[2] * 8 + at[0] * 2 + core) * tdev + row % tdev
        match = names == IDR[...]
        t = slope * scores + shift
        t = jnp.where(match, -t, t)
        top = jnp.where(match, -scale, scale)
        weights = (top / (1.0 + jnp.exp2(t))).astype(jnp.bfloat16)
        GT[r[0], r[1], r[2]] = (
            jnp.dot(weights, images, preferred_element_type=jnp.float32)
            .astype(jnp.bfloat16)
            .reshape(2, 2, 2, tdev, 3 * third)
        )
        each_heavy(n, lambda p, half: heavy_reduce(p, n, half).start())
        W[pl.ds(pl.multiple_of((7 - n) * chunk, chunk), chunk), :] = weights

        @pl.when(n >= lag)
        def _():
            take_in(n - lag)

        return 0

    lax.fori_loop(0, 8, body, 0)

    step = block
    swaps = [
        remote(
            GI.at[pl.ds(rows + i * step, step)], RB.at[pl.ds(i * step, step)],
            gi_send.at[i], gi_recv.at[i], sibling,
        )
        for i in range(pieces)
    ]

    def finish(i):
        swaps[i].wait_recv()
        at = pl.ds(i * step, step)
        gi_out[at, :] = RB[at, :] + GI[at, :]

    for i in range(pieces):
        image_block(pieces + i)
        swaps[i].start()
        if i in (0, 2):
            take_in(6 + i // 2)
    image_block(0, 2)
    ends = []
    for p, (a1, a2, a3) in enumerate(ORDERS):
        for par in (0, 1):
            for e in (1, 2, 3):
                pltpu.make_async_copy(
                    R2.at[p, e - 1, par], R2.at[p, e - 1, par], r2_recv.at[p, par, e - 1]
                ).wait()
        for e in (2, 1, 3, 0):
            total = S1[p, 0, 0, e % 2, e // 2].astype(jnp.float32)
            for k in range(3):
                total += R2[p, k, e % 2, e // 2].astype(jnp.float32)
            if e:
                S2[p, e - 1] = total.astype(jnp.bfloat16)
                cp = remote(
                    S2.at[p, e - 1], R3.at[p, e - 1],
                    r3_send.at[p, e - 1], r3_recv.at[p, e - 1], shifted(a1, e),
                )
                cp.start()
                ends.append((p, e, cp))
            else:
                gt_out[:, pl.ds(p * third, third)] = total
    for i in range(2):
        finish(i)
    image_block(2, 2)
    for i in range(2, pieces):
        finish(i)
    for p, e, cp in ends:
        cp.wait_recv()
    for p in range(3):
        cols = pl.ds(p * third, third)
        total = gt_out[:, cols]
        for k in range(3):
            total += R3[p, k].astype(jnp.float32)
        gt_out[:, cols] = total

    for cp in [send_v, send_ids] + swaps + [cp for _, _, cp in ends]:
        cp.wait_send()
    for p, (a1, a2, a3) in enumerate(ORDERS):
        for e in (1, 2, 3):
            light_gather(p, e).wait_send()
            for low in (0, 1):
                middle_gather(p, low, e).wait_send()
        for n in range(8):
            odd = parities(n)[a3]
            for half in (0, 1):
                (heavy_gather if odd else pass_on)(p, n, half).wait_send()
                if odd + 2 * half:
                    heavy_reduce(p, n, half).wait_send()
    for p, (a1, a2, a3) in enumerate(ORDERS):
        for low in (0, 1):
            for e in (1, 2, 3):
                q = put(a1, low, put(a2, e % 2, (0, 0, 0)))
                middle_reduce(p, q, e // 2).wait_send()


def shards(images, texts, partners, scale, bias):
    rows, width = images.shape
    tdev = texts.shape[0]
    third = width // 3
    vmem = pltpu.VMEM
    sem = pltpu.SemaphoreType.DMA
    pieces = 4
    gathered = (2, 2, 2, 2, 2, 2, tdev, width)
    return pl.pallas_call(
        functools.partial(kernel, 2),
        out_shape=(
            pltpu.VMEM((rows, width), jnp.float32),
            pltpu.VMEM((tdev, width), jnp.float32),
        ),
        in_specs=[
            pl.BlockSpec(memory_space=pltpu.SMEM),
            pl.BlockSpec(memory_space=pltpu.SMEM),
            pl.BlockSpec(memory_space=pltpu.VMEM),
            pl.BlockSpec(memory_space=pltpu.HBM),
            pl.BlockSpec(memory_space=pltpu.HBM),
        ],
        out_specs=(pl.BlockSpec(memory_space=pltpu.VMEM), pl.BlockSpec(memory_space=pltpu.VMEM)),
        scratch_shapes=[
            vmem((2 * rows, width), jnp.bfloat16),
            vmem(gathered, jnp.bfloat16),
            vmem((64 * tdev, 2 * rows), jnp.bfloat16),
            vmem((2 * rows, width), jnp.float32),
            vmem(gathered, jnp.bfloat16),
            vmem((rows, width), jnp.float32),
            vmem((3, 3, 2, 2, 2, 2, tdev, third), jnp.bfloat16),
            vmem((3, 2, 2, 2, 2, tdev, third), jnp.bfloat16),
            vmem((3, 3, 2, 2, tdev, third), jnp.bfloat16),
            vmem((3, 3, tdev, third), jnp.bfloat16),
            vmem((3, 3, tdev, third), jnp.bfloat16),
            vmem((rows // 128, 128), jnp.int32),
            vmem((1, 2 * rows), jnp.int32),
            sem((2,)), sem, sem, sem, sem, sem((pieces,)), sem((pieces,)),
            sem((3, 3)), sem((3, 3)), sem((3, 2, 3)), sem((3, 2, 3)), sem((3, 8, 2)), sem((3, 8, 2)),
            sem((3, 8, 2)), sem((3, 8, 2)), sem((3, 2, 3)), sem((3, 2, 3)), sem((3, 3)), sem((3, 3)),
        ],
        compiler_params=pltpu.CompilerParams(
            collective_id=0, has_side_effects=True, vmem_limit_bytes=52 * 2**20
        ),
        cost_estimate=pl.CostEstimate(
            flops=3 * 2 * 2 * rows * 64 * tdev * width, bytes_accessed=8 * rows * width, transcendentals=0
        ),
    )(
        scale.reshape(1, 1), bias.reshape(1, 1), partners.reshape(rows // 128, 128), images, texts
    )


def solution(mesh):
    return jax.shard_map(
        shards,
        mesh=mesh,
        in_specs=(P(AXES, None), P(AXES, None), P(AXES), P(), P()),
        out_specs=(P(AXES, None), P(AXES, None)),
        check_vma=False,
    )
```
